32 devices in a mesh: band: 8 (over z, x), lev: 4 (over y, core).
Axes of the slice: x: 2, y: 2, z: 4, core: 2. Of those that a mesh axis runs over, the one named last changes fastest.
Arguments:
- spectral: bfloat16 [4, 32, 640, 640], P(None, 'lev', 'band'), may hold values from -6 to 6
- legendre_value: bfloat16 [640, 8, 640], P('band'), may hold values from -0.009765625 to 0.009765625
- legendre_slope: bfloat16 [640, 8, 640], P('band'), may hold values from -0.009765625 to 0.009765625
- wave_numbers: int32 [640], replicated, may hold values from 0 to 639, each once
- aerosol_old: bfloat16 [40, 32, 8, 2688], P(None, 'lev', 'band'), may hold values from 0 to 2
- vertical_weight: bfloat16 [3, 32, 8, 2688], P(None, 'lev', 'band'), may hold values from 0 to 0.59765625
- send_blocks: int32 [8, 5, 4], P('band'), may hold values from -1 to 20, as said below
- depart_slot: int32 [168, 4], P('band'), may hold values from 0 to 19, as said below
- depart_offset: int32 [168, 4, 128], P('band'), may hold values from 0 to 124
- depart_weight: bfloat16 [168, 4, 4, 128], P('band'), may hold values from 0 to 0.5
Outputs:
- wind_grid: bfloat16 [2, 32, 8, 2688], P(None, 'lev', 'band')
- aerosol_new: bfloat16 [40, 32, 8, 2688], P(None, 'lev', 'band')
- aerosol_flux: bfloat16 [2, 32, 8, 2688], P(None, 'lev', 'band')
The draws below stay inside these ranges and needn't reach their ends.
Inputs may be any that keep to these rules, and one draw needn't show every extreme that they name: `send_blocks`: row b, offset o lists up to 4 of band b's own blocks (block l * 21 + c is the band's latitude l, longitudes c * 128 onward) that band b + o - 2 reads; -1 marks an empty slot; offsets toward bands that do not exist are empty; some rows are full. `depart_slot`: slot o * 4 + e of band r's pool is what band r - o + 2 lists at offset o, slot e; arrival block g belongs to band g // 21 and every slot it names is filled.
All inputs are finite; a program needn't handle non-finite values.
Results may differ from the reference program's by a relative error of at most 0.0062.
Values may be sent and summed in bfloat16 or wider, within the bound.
A program may use at most 128 MiB of HBM per device.

```python
import math
import jax
import jax.numpy as jnp
from jax import lax

WAVES = 640
TRUNC = 640
BINS = 40
NLON = 2688
BLK = 128
STENCIL = 4
REACH = 2
CAP = 4
LAT_DEV = 1
LEVELS = 32
NLAT = 8
NBL = 21
NB = 21
NBLK = 168
OFFS = 5


def routing_tables(key):
    band_count = NLAT // LAT_DEV
    count_key = jax.random.fold_in(key, 101)
    block_key = jax.random.fold_in(key, 202)
    pick_key = jax.random.fold_in(key, 303)
    band_rows = jnp.arange(band_count, dtype=jnp.int32)[:, None]
    offsets = jnp.arange(OFFS, dtype=jnp.int32)[None, :]
    targets = band_rows + offsets - REACH
    inside = (targets >= 0) & (targets < band_count)
    near_pole = (band_rows <= 2 * REACH) | (band_rows >= band_count - 1 - 2 * REACH)
    counts = jax.random.randint(count_key, (band_count, OFFS), 1, CAP + 1)
    counts = jnp.where(near_pole, CAP, counts)
    counts = jnp.where(inside, counts, 0)
    slot_number = jnp.arange(CAP, dtype=jnp.int32)
    filled = slot_number[None, None, :] < counts[:, :, None]
    chosen = jax.random.randint(block_key, (band_count, OFFS, CAP), 0, NB)
    chosen = chosen.at[:, REACH, 0].set(NB - 1)
    listed = jnp.where(filled, chosen, -1)
    senders = band_rows - offsets + REACH
    sender_valid = (senders >= 0) & (senders < band_count)
    pool_filled = filled[jnp.clip(senders, 0, band_count - 1), offsets] & sender_valid[:, :, None]
    pool_filled = pool_filled.reshape(band_count, OFFS * CAP).astype(jnp.int32)
    live_count = jnp.sum(pool_filled, axis=1)
    slot_ranks = jnp.cumsum(pool_filled, axis=1) - 1
    random_bits = jax.random.randint(pick_key, (band_count, NB, STENCIL), 0, 1 << 20)
    wanted = random_bits % live_count[:, None, None]
    wanted = wanted.at[:, 0, 0].set(live_count - 1)
    wanted = wanted.at[:, 0, 1].set(0)
    matches = (slot_ranks[:, None, None, :] == wanted[:, :, :, None]) & (pool_filled[:, None, None, :] == 1)
    picked = jnp.argmax(matches.astype(jnp.int32), axis=-1).astype(jnp.int32)
    return (listed.astype(jnp.int32), picked.reshape(band_count * NB, STENCIL))


def draw_send_blocks(key, part):
    listed, picked = routing_tables(key)
    return listed


def draw_depart_slot(key, part):
    listed, picked = routing_tables(key)
    return picked


def set_ends(array, own_key, smallest, top_value):
    longest = array.shape.index(max(array.shape))
    spots = []
    for shift in (0, 1):
        where = [jax.random.randint(jax.random.fold_in(own_key, axis), (), 0, length) for axis, length in enumerate(array.shape)]
        where[longest] = (where[longest] + shift) % array.shape[longest]
        spots.append(tuple(where))
    return array.at[spots[0]].set(smallest).at[spots[1]].set(top_value)


def steps_of(key, shape, split, smallest, top_value):
    def one(axis_at, shards_of):
        steps = jax.random.uniform(jax.random.fold_in(jax.random.fold_in(key, 6), axis_at), (shards_of,), jnp.float32, smallest / len(split), top_value / len(split))
        return jnp.repeat(jnp.exp(steps), shape[axis_at] // shards_of).reshape((-1,) + (1,) * (len(shape) - axis_at - 1))

    gain = one(*split[0])
    for cut in split[1:]:
        gain = gain * one(*cut)
    return gain


def scatter_about(key, dims, scale, reach, shards=(), held_as=jnp.bfloat16):
    entries = jax.random.normal(key, dims, jnp.float32) * scale
    if len(shards) > 0:
        entries = steps_of(key, dims, shards, -0.22, 0.18) * entries
    return jnp.clip(entries, min=-reach, max=reach).astype(held_as)


def setup_inputs(seed: int = 0) -> dict:
    key_of = jax.random.split(jax.random.key(seed), 11)
    spectral = scatter_about(key_of[0], (4, LEVELS, WAVES, TRUNC), 1.0, 6.0, ((1, 4), (2, 8)))
    legendre_value = scatter_about(key_of[1], (WAVES, NLAT, TRUNC), (TRUNC * WAVES) ** -0.5, 0.009765625, ((0, 8),))
    legendre_slope = scatter_about(key_of[2], (WAVES, NLAT, TRUNC), (TRUNC * WAVES) ** -0.5, 0.009765625, ((0, 8),))
    wave_numbers = jax.random.permutation(key_of[3], WAVES).astype(jnp.int32)
    aerosol_old = jnp.clip(2.0 * jax.random.uniform(key_of[4], (BINS, LEVELS, NLAT, NLON), jnp.float32) ** steps_of(key_of[4], (BINS, LEVELS, NLAT, NLON), ((1, 4), (2, 8)), -0.2, 0.2), 0.0, 2.0).astype(jnp.bfloat16)
    vertical_weight = jnp.clip(0.59765625 * jax.random.uniform(key_of[5], (3, LEVELS, NLAT, NLON), jnp.float32) ** steps_of(key_of[5], (3, LEVELS, NLAT, NLON), ((1, 4), (2, 8)), -0.2, 0.2), 0.0, 0.59765625).astype(jnp.bfloat16)
    send_blocks = draw_send_blocks(jax.random.fold_in(key_of[10], 71), 0)
    depart_slot = draw_depart_slot(jax.random.fold_in(key_of[10], 71), 0)
    depart_offset = set_ends(jax.random.randint(key_of[8], (NBLK, STENCIL, BLK), 0, BLK - STENCIL + 1), jax.random.fold_in(key_of[8], 1), 0, BLK - STENCIL).astype(jnp.int32)
    depart_weight = jnp.clip(0.5 * jax.random.uniform(key_of[9], (NBLK, STENCIL, STENCIL, BLK), jnp.float32) ** steps_of(key_of[9], (NBLK, STENCIL, STENCIL, BLK), ((0, 8),), -0.2, 0.2), 0.0, 0.5).astype(jnp.bfloat16)
    return {"spectral": spectral, "legendre_value": legendre_value, "legendre_slope": legendre_slope, "wave_numbers": wave_numbers, "aerosol_old": aerosol_old, "vertical_weight": vertical_weight, "send_blocks": send_blocks, "depart_slot": depart_slot, "depart_offset": depart_offset, "depart_weight": depart_weight}


def fourier_table(wave_numbers, lon_count):
    longitudes = jnp.arange(lon_count, dtype=jnp.int32)
    phases = (wave_numbers[:, None] * longitudes[None, :]) % lon_count
    angles = phases.astype(jnp.float32) * (2.0 * math.pi / lon_count)
    doubled = jnp.where(wave_numbers == 0, 1.0, 2.0).astype(jnp.float32)[:, None]
    return jnp.stack([doubled * jnp.cos(angles), -doubled * jnp.sin(angles)]).astype(jnp.bfloat16)


def stencil_matrix(depart_offset, depart_weight):
    width = depart_offset.shape[-1]
    columns = jnp.arange(width, dtype=jnp.int32)
    summed = jnp.zeros(depart_offset.shape[:2] + (width, width), jnp.float32)
    for term_index in range(depart_weight.shape[2]):
        matches = columns[None, None, :, None] == (depart_offset[:, :, None, :] + term_index)
        summed = summed + jnp.where(matches, depart_weight[:, :, term_index, None, :].astype(jnp.float32), 0.0)
    return summed


def reference(spectral, legendre_value, legendre_slope, wave_numbers, aerosol_old, vertical_weight, send_blocks, depart_slot, depart_offset, depart_weight):
    spectral_wide = spectral.astype(jnp.float32)
    value_terms = jnp.einsum('slj,xksj->xkls', legendre_value.astype(jnp.float32), spectral_wide)
    slope_terms = jnp.einsum('slj,xksj->xkls', legendre_slope.astype(jnp.float32), spectral_wide)
    factor = wave_numbers.astype(jnp.float32) / WAVES
    coefficients = jnp.stack([
        -slope_terms[0] - factor * value_terms[3],
        -slope_terms[1] + factor * value_terms[2],
        slope_terms[2] - factor * value_terms[1],
        slope_terms[3] + factor * value_terms[0]]).astype(jnp.bfloat16)
    fourier = fourier_table(wave_numbers, NLON)
    paired = coefficients.astype(jnp.float32).reshape(2, 2, LEVELS, NLAT, WAVES)
    wind_grid = jnp.einsum('wxklm,xmi->wkli', paired, fourier.astype(jnp.float32)).astype(jnp.bfloat16)

    weights = vertical_weight.astype(jnp.float32)

    def remap_bin(column):
        padded = jnp.pad(column.astype(jnp.float32), ((1, 1), (0, 0), (0, 0)))
        return (weights[0] * padded[:-2] + weights[1] * padded[1:-1] + weights[2] * padded[2:]).astype(jnp.bfloat16)

    remapped = lax.map(remap_bin, aerosol_old)
    blocks = remapped.reshape(BINS, LEVELS, NBLK, BLK).transpose(2, 0, 1, 3).reshape(NBLK, BINS * LEVELS, BLK)
    band_count = NLAT // LAT_DEV
    band_rows = jnp.arange(band_count, dtype=jnp.int32)[:, None]
    offsets = jnp.arange(OFFS, dtype=jnp.int32)[None, :]
    senders = jnp.clip(band_rows - offsets + REACH, 0, band_count - 1)
    listed = send_blocks[senders, offsets]
    global_ids = (senders[:, :, None] * NB + jnp.clip(listed, 0, NB - 1)).reshape(band_count, OFFS * CAP)
    owners = jnp.arange(NBLK, dtype=jnp.int32) // NB
    source_block = global_ids[owners[:, None], depart_slot]

    def one_band(inputs):
        sources, shifts, stencil_weights = inputs
        chosen = blocks[sources].astype(jnp.float32)
        stencil = stencil_matrix(shifts, stencil_weights)
        return jnp.einsum('jifq,jiqp->jfp', chosen, stencil).astype(jnp.bfloat16)

    results = lax.map(one_band, (source_block.reshape(band_count, NB, STENCIL),
                                 depart_offset.reshape(band_count, NB, STENCIL, BLK),
                                 depart_weight.reshape(band_count, NB, STENCIL, STENCIL, BLK)))
    aerosol_new = results.reshape(NLAT, NBL, BINS, LEVELS, BLK).transpose(2, 3, 0, 1, 4).reshape(BINS, LEVELS, NLAT, NLON)
    average = jnp.mean(aerosol_new.astype(jnp.float32), axis=0)
    aerosol_flux = (wind_grid.astype(jnp.float32) * average[None]).astype(jnp.bfloat16)
    return (wind_grid, aerosol_new, aerosol_flux)
```

```python
import functools
import math

import jax
import jax.numpy as jnp
from jax import lax
from jax.experimental import pallas as pl
from jax.experimental.pallas import tpu as pltpu
from jax.sharding import PartitionSpec as P

WAVES = 640
NLON = 2688
BLK = 128
GROUP = 16
LANES = 128
LIMIT = 48 * 2**20
VMEM = pl.BlockSpec(memory_space=pltpu.VMEM)
SMEM = pl.BlockSpec(memory_space=pltpu.SMEM)


def shifted(value, axis, steps):
    count = lax.axis_size(axis)
    leading, last = (max(0, -steps), min(count, count - steps))
    return lax.ppermute(value, axis, [(source, source + steps) for source in range(leading, last)])


def padded_to(value, axis, multiple):
    extra = -value.shape[axis] % multiple
    if extra == 0:
        return value
    widths = [(0, 0)] * value.ndim
    widths[axis] = (0, extra)
    return jnp.pad(value, widths)


def legendre_kernel(lat_count, level_count, spec_ref, val_ref, slope_ref, factor_ref, out_ref, acc):
    step = pl.program_id(0)
    rows = spec_ref.shape[0]
    cols = GROUP * lat_count
    spec = spec_ref[...].reshape(rows * GROUP, spec_ref.shape[2])
    own = lax.broadcasted_iota(jnp.int32, (GROUP, cols), 0)
    col = lax.broadcasted_iota(jnp.int32, (GROUP, cols), 1)
    keep = (col // lat_count == own)[None]

    def terms(table_ref):
        table = table_ref[...].reshape(cols, table_ref.shape[2])
        product = lax.dot_general(
            spec, table, (((1,), (1,)), ((), ())), preferred_element_type=jnp.float32
        )
        product = product.reshape(rows, GROUP, cols)
        return jnp.sum(jnp.where(keep, product, 0.0), axis=1)

    value = terms(val_ref)
    slope = terms(slope_ref)
    factor = factor_ref[0]
    k = level_count
    v = [value[x * k : (x + 1) * k] for x in range(4)]
    d = [slope[x * k : (x + 1) * k] for x in range(4)]
    coefficients = jnp.concatenate(
        [
            -d[0] - factor * v[3],
            -d[1] + factor * v[2],
            d[2] - factor * v[1],
            d[3] + factor * v[0],
        ],
        axis=0,
    ).astype(jnp.bfloat16)
    width = acc.shape[1]
    lanes = width // lat_count
    row = lax.broadcasted_iota(jnp.int32, (cols, width), 0)
    lane = lax.broadcasted_iota(jnp.int32, (cols, width), 1)
    slot = lane % lanes - step * GROUP
    hot = ((slot * lat_count + lane // lanes == row) & (slot >= 0) & (slot < GROUP)).astype(
        jnp.float32
    ).astype(jnp.bfloat16)
    part = jnp.dot(coefficients, hot, preferred_element_type=jnp.float32)

    @pl.when(step == 0)
    def _():
        acc[...] = part

    @pl.when(step > 0)
    def _():
        acc[...] += part

    @pl.when(step == pl.num_programs(0) - 1)
    def _():
        for lat in range(lat_count):
            out_ref[lat] = acc[:, lat * lanes : (lat + 1) * lanes].astype(jnp.bfloat16)


def wind_coefficients(spectral, legendre_value, legendre_slope, own_waves):
    fields, level_count, wave_local, trunc = spectral.shape
    lat_count = legendre_value.shape[1]
    rows = fields * level_count
    spec = padded_to(spectral.reshape(rows, wave_local, trunc), 1, GROUP)
    value = padded_to(legendre_value, 0, GROUP)
    slope = padded_to(legendre_slope, 0, GROUP)
    steps = spec.shape[1] // GROUP
    lanes = -(-spec.shape[1] // LANES) * LANES
    factor = padded_to(own_waves.astype(jnp.float32) / WAVES, 0, GROUP)
    factor = jnp.broadcast_to(factor[:, None], (factor.shape[0], lat_count))
    factor = factor.reshape(steps, 1, GROUP * lat_count)
    table = pl.BlockSpec((GROUP, lat_count, trunc), lambda g: (g, 0, 0))
    return pl.pallas_call(
        functools.partial(legendre_kernel, lat_count, level_count),
        out_shape=jax.ShapeDtypeStruct((lat_count, rows, lanes), jnp.bfloat16),
        grid=(steps,),
        in_specs=[
            pl.BlockSpec((rows, GROUP, trunc), lambda g: (0, g, 0)),
            table,
            table,
            pl.BlockSpec((1, 1, GROUP * lat_count), lambda g: (g, 0, 0)),
        ],
        out_specs=pl.BlockSpec((lat_count, rows, lanes), lambda g: (0, 0, 0)),
        scratch_shapes=[pltpu.VMEM((rows, lat_count * lanes), jnp.float32)],
        compiler_params=pltpu.CompilerParams(vmem_limit_bytes=LIMIT),
        cost_estimate=pl.CostEstimate(
            flops=2 * rows * GROUP * 2 * GROUP * lat_count * trunc * steps,
            bytes_accessed=5_000_000,
            transcendentals=0,
        ),
    )(spec, value, slope, factor)


def wind_kernel(received_ref, cos_block_ref, sin_block_ref, table_ref, wind_ref, lhs):
    shard_count = received_ref.shape[0]
    level_count = wind_ref.shape[1]
    k = level_count
    whole = jnp.concatenate([received_ref[b] for b in range(shard_count)], axis=1)
    whole = whole.astype(jnp.float32)
    real = jnp.concatenate([whole[0:k], whole[2 * k : 3 * k]], axis=0)
    imag = jnp.concatenate([whole[k : 2 * k], whole[3 * k : 4 * k]], axis=0)
    width = whole.shape[1]
    block_count = cos_block_ref.shape[0]
    for c in range(block_count):
        cos_c = cos_block_ref[c : c + 1, :]
        sin_c = sin_block_ref[c : c + 1, :]
        at = slice(c * 2 * k, (c + 1) * 2 * k)
        lhs[at, 0:width] = (real * cos_c - imag * sin_c).astype(jnp.bfloat16)
        lhs[at, width : 2 * width] = (-real * sin_c - imag * cos_c).astype(jnp.bfloat16)
    grid = jnp.dot(lhs[...], table_ref[...], preferred_element_type=jnp.float32)
    grid = grid.astype(jnp.bfloat16)
    for c in range(block_count):
        for w in range(2):
            start = (2 * c + w) * k
            wind_ref[w, :, c * BLK : (c + 1) * BLK] = grid[start : start + k]


def angle_tables(wave_numbers, shard_count, lanes, block_count):
    waves = padded_to(wave_numbers.reshape(shard_count, -1), 1, lanes).reshape(-1)
    scale = 2.0 * math.pi / NLON
    doubled = jnp.where(waves == 0, 1.0, 2.0).astype(jnp.float32)
    starts = jnp.arange(block_count, dtype=jnp.int32) * BLK
    coarse = (starts[:, None] * waves[None, :] % NLON).astype(jnp.float32) * scale
    fine = jnp.arange(BLK, dtype=jnp.int32)
    fine = (waves[:, None] * fine[None, :] % NLON).astype(jnp.float32) * scale
    table = jnp.concatenate([jnp.cos(fine), jnp.sin(fine)], axis=0).astype(jnp.bfloat16)
    return doubled * jnp.cos(coarse), doubled * jnp.sin(coarse), table


def winds(received, cos_block, sin_block, table, level_count, lon_count):
    block_count = lon_count // BLK
    width = table.shape[0]
    return pl.pallas_call(
        wind_kernel,
        out_shape=jax.ShapeDtypeStruct((2, level_count, lon_count), jnp.bfloat16),
        in_specs=[VMEM] * 4,
        out_specs=VMEM,
        scratch_shapes=[pltpu.VMEM((block_count * 2 * level_count, width), jnp.bfloat16)],
        compiler_params=pltpu.CompilerParams(vmem_limit_bytes=LIMIT),
        cost_estimate=pl.CostEstimate(
            flops=2 * block_count * 2 * level_count * width * BLK,
            bytes_accessed=2_000_000,
            transcendentals=0,
        ),
    )(received, cos_block, sin_block, table)


def remap_kernel(offsets, slots, listed_ref, old_ref, below_ref, above_ref, weight_ref, *out_refs):
    level_count = old_ref.shape[1]
    block_count = old_ref.shape[2] // BLK
    level = lax.broadcasted_iota(jnp.int32, (1, level_count, BLK), 1)
    for o in range(offsets):
        for e in range(slots):
            block = jnp.clip(listed_ref[o * slots + e], 0, block_count - 1)
            lons = pl.ds(pl.multiple_of(block * BLK, BLK), BLK)
            weights = weight_ref[:, :, lons].astype(jnp.float32)
            old = old_ref[:, :, lons].astype(jnp.float32)
            below = below_ref[:, :, lons].astype(jnp.float32)
            above = above_ref[:, :, lons].astype(jnp.float32)
            lower = jnp.where(level == 0, below, pltpu.roll(old, 1, 1))
            upper = jnp.where(
                level == level_count - 1, above, pltpu.roll(old, level_count - 1, 1)
            )
            summed = weights[0:1] * lower + weights[1:2] * old + weights[2:3] * upper
            out_refs[o][e] = summed.astype(jnp.bfloat16)


def remapped_blocks(listed, old, below, above, weight):
    offsets, slots = listed.shape
    bin_count, level_count, _ = old.shape
    piece = jax.ShapeDtypeStruct((slots, bin_count, level_count, BLK), jnp.bfloat16)
    return pl.pallas_call(
        functools.partial(remap_kernel, offsets, slots),
        out_shape=[piece] * offsets,
        in_specs=[SMEM] + [VMEM] * 4,
        out_specs=[VMEM] * offsets,
        compiler_params=pltpu.CompilerParams(vmem_limit_bytes=LIMIT),
        cost_estimate=pl.CostEstimate(
            flops=10 * old.size, bytes_accessed=4_000_000, transcendentals=0
        ),
    )(listed.reshape(-1), old, below, above, weight)


def arrive_kernel(offsets, slots, depart_ref, start_ref, weight_ref, wind_ref, *refs):
    pool_refs = refs[:offsets]
    new_ref, flux_ref, pool = refs[offsets:]
    block = pl.program_id(0)
    bin_count, level_count, width = new_ref.shape
    rows = bin_count * level_count

    @pl.when(block == 0)
    def _():
        for o in range(offsets):
            for e in range(slots):
                pool[o * slots + e] = pool_refs[o][e].reshape(rows, width)

    stencil_rows = start_ref.shape[1]
    points = weight_ref.shape[2]
    q = lax.broadcasted_iota(jnp.int32, (width, width), 0)
    taken, matrices = [], []
    for t in range(stencil_rows):
        away = q - start_ref[0, t : t + 1, :]
        weights = weight_ref[0, t].astype(jnp.float32)
        matrix = jnp.zeros((width, width), jnp.float32)
        for u in range(points):
            matrix = jnp.where(away == u, weights[u : u + 1, :], matrix)
        matrices.append(matrix.astype(jnp.bfloat16))
        taken.append(pool[depart_ref[block * stencil_rows + t]])
    lhs = jnp.concatenate(taken, axis=1)
    rhs = jnp.concatenate(matrices, axis=0)
    new = jnp.dot(lhs, rhs, preferred_element_type=jnp.float32).astype(jnp.bfloat16)
    new = new.reshape(bin_count, level_count, width)
    new_ref[...] = new
    average = jnp.sum(new.astype(jnp.float32), axis=0) / bin_count
    flux_ref[...] = (wind_ref[...].astype(jnp.float32) * average[None]).astype(jnp.bfloat16)


def arrivals(depart_slot, depart_offset, depart_weight, wind, pieces):
    offsets = len(pieces)
    slots, bin_count, level_count, _ = pieces[0].shape
    block_count, stencil_rows = depart_slot.shape
    lon_count = wind.shape[2]
    rows = bin_count * level_count
    points = depart_weight.shape[2]
    two = pl.BlockSpec((2, level_count, BLK), lambda c: (0, 0, c))
    return pl.pallas_call(
        functools.partial(arrive_kernel, offsets, slots),
        out_shape=[
            jax.ShapeDtypeStruct((bin_count, level_count, lon_count), jnp.bfloat16),
            jax.ShapeDtypeStruct((2, level_count, lon_count), jnp.bfloat16),
        ],
        grid=(block_count,),
        in_specs=[
            SMEM,
            pl.BlockSpec((1, stencil_rows, BLK), lambda c: (c, 0, 0)),
            pl.BlockSpec((1, stencil_rows, points, BLK), lambda c: (c, 0, 0, 0)),
            two,
        ]
        + [VMEM] * offsets,
        out_specs=[pl.BlockSpec((bin_count, level_count, BLK), lambda c: (0, 0, c)), two],
        scratch_shapes=[pltpu.VMEM((offsets * slots, rows, BLK), jnp.bfloat16)],
        compiler_params=pltpu.CompilerParams(vmem_limit_bytes=LIMIT),
        cost_estimate=pl.CostEstimate(
            flops=2 * block_count * stencil_rows * rows * BLK * BLK,
            bytes_accessed=4_000_000,
            transcendentals=0,
        ),
    )(depart_slot.reshape(-1), depart_offset, depart_weight, wind, *pieces)


def shards(
    spectral,
    legendre_value,
    legendre_slope,
    wave_numbers,
    aerosol_old,
    vertical_weight,
    send_blocks,
    depart_slot,
    depart_offset,
    depart_weight,
):
    band_here = lax.axis_index("band")
    band_count = lax.axis_size("band")
    wave_local = spectral.shape[2]
    bin_count, level_count, lat_count, lon_count = aerosol_old.shape
    old = aerosol_old.reshape(bin_count, level_count, lon_count)
    weight = vertical_weight.reshape(3, level_count, lon_count)
    below = shifted(old[:, level_count - 1 :], "lev", 1)
    above = shifted(old[:, :1], "lev", -1)

    own_waves = lax.dynamic_slice_in_dim(wave_numbers, band_here * wave_local, wave_local, 0)
    coefficients = wind_coefficients(spectral, legendre_value, legendre_slope, own_waves)
    received = lax.all_to_all(coefficients, "band", split_axis=0, concat_axis=0, tiled=True)
    cos_block, sin_block, table = angle_tables(
        wave_numbers, band_count, coefficients.shape[2], lon_count // BLK
    )

    outgoing = remapped_blocks(send_blocks[0], old, below, above, weight)
    reach_bands = len(outgoing) // 2
    pieces = [
        piece if index == reach_bands else shifted(piece, "band", index - reach_bands)
        for index, piece in enumerate(outgoing)
    ]
    wind = winds(received, cos_block, sin_block, table, level_count, lon_count)
    new, flux = arrivals(depart_slot, depart_offset, depart_weight, wind, pieces)
    lat_shape = (level_count, lat_count, lon_count)
    return (
        wind.reshape((2, *lat_shape)),
        new.reshape((bin_count, *lat_shape)),
        flux.reshape((2, *lat_shape)),
    )


def solution(mesh):
    return jax.shard_map(
        shards,
        mesh=mesh,
        in_specs=(
            P(None, "lev", "band", None),
            P("band", None, None),
            P("band", None, None),
            P(),
            P(None, "lev", "band", None),
            P(None, "lev", "band", None),
            P("band", None, None),
            P("band", None),
            P("band", None, None),
            P("band", None, None, None),
        ),
        out_specs=(
            P(None, "lev", "band", None),
            P(None, "lev", "band", None),
            P(None, "lev", "band", None),
        ),
        check_vma=False,
    )
```

```python
import functools
import math

import jax
import jax.numpy as jnp
from jax import lax
from jax.experimental import pallas as pl
from jax.experimental.pallas import tpu as pltpu
from jax.sharding import PartitionSpec as P

WAVES = 640
NLON = 2688
BLK = 128
GROUP = 16
LANES = 128
LIMIT = 48 * 2**20
VMEM = pl.BlockSpec(memory_space=pltpu.VMEM)
SMEM = pl.BlockSpec(memory_space=pltpu.SMEM)


ANY = pl.BlockSpec(memory_space=pl.ANY)
MESH = pl.DeviceIdType.MESH


def padded_to(value, axis, multiple):
    extra = -value.shape[axis] % multiple
    if extra == 0:
        return value
    widths = [(0, 0)] * value.ndim
    widths[axis] = (0, extra)
    return jnp.pad(value, widths)


def angle_tables(wave_numbers, shard_count, lanes, block_count):
    waves = padded_to(wave_numbers.reshape(shard_count, -1), 1, lanes).reshape(-1)
    scale = 2.0 * math.pi / NLON
    doubled = jnp.where(waves == 0, 1.0, 2.0).astype(jnp.float32)
    starts = jnp.arange(block_count, dtype=jnp.int32) * BLK
    coarse = (starts[:, None] * waves[None, :] % NLON).astype(jnp.float32) * scale
    fine = jnp.arange(BLK, dtype=jnp.int32)
    fine = (waves[:, None] * fine[None, :] % NLON).astype(jnp.float32) * scale
    table = jnp.concatenate([jnp.cos(fine), jnp.sin(fine)], axis=0).astype(jnp.bfloat16)
    return doubled * jnp.cos(coarse), doubled * jnp.sin(coarse), table


def block_of(index):
    return pl.ds(pl.multiple_of(index * BLK, BLK), BLK)


def gather_kernel(listed_ref, old_ref, weight_ref, blocks_ref, weights_ref):
    block_count = old_ref.shape[2] // BLK

    def take(slot, carry):
        lons = block_of(jnp.clip(listed_ref[slot], 0, block_count - 1))
        blocks_ref[slot] = old_ref[:, :, lons]
        weights_ref[slot] = weight_ref[:, :, lons]
        return carry

    lax.fori_loop(0, blocks_ref.shape[0], take, 0)


def listed_blocks(listed, old, weight):
    count = listed.shape[0]
    bins, k, _ = old.shape
    return pl.pallas_call(
        gather_kernel,
        out_shape=[
            jax.ShapeDtypeStruct((count, bins, k, BLK), jnp.bfloat16),
            jax.ShapeDtypeStruct((count, 3, k, BLK), jnp.bfloat16),
        ],
        in_specs=[SMEM, VMEM, VMEM],
        out_specs=[VMEM, VMEM],
        compiler_params=pltpu.CompilerParams(vmem_limit_bytes=LIMIT),
    )(listed, old, weight)


def arrive_kernel(depart_ref, stencil_ref, wind_ref, pool_ref, new_ref, flux_ref):
    bins, k, lon_count = new_ref.shape
    block_count, depth, _ = stencil_ref.shape
    stencil_rows = depth // BLK

    def arrive(c, carry):
        taken = [pool_ref[depart_ref[c * stencil_rows + t]] for t in range(stencil_rows)]
        new = jnp.dot(
            jnp.concatenate(taken, axis=1), stencil_ref[c], preferred_element_type=jnp.float32
        )
        new = new.astype(jnp.bfloat16).astype(jnp.float32).reshape(bins, k, BLK)
        lons = block_of(c)
        new_ref[:, :, lons] = new.astype(jnp.bfloat16)
        average = jnp.sum(new, axis=0) / bins
        wind = wind_ref[:, :, lons].astype(jnp.float32)
        flux_ref[:, :, lons] = (wind * average[None]).astype(jnp.bfloat16)
        return carry

    lax.fori_loop(0, block_count, arrive, 0)


def arrivals(depart_slot, stencil, wind, pool, bins):
    _, k, lon_count = wind.shape
    return pl.pallas_call(
        arrive_kernel,
        out_shape=[
            jax.ShapeDtypeStruct((bins, k, lon_count), jnp.bfloat16),
            jax.ShapeDtypeStruct((2, k, lon_count), jnp.bfloat16),
        ],
        in_specs=[SMEM] + [VMEM] * 3,
        out_specs=[VMEM, VMEM],
        compiler_params=pltpu.CompilerParams(vmem_limit_bytes=LIMIT),
        cost_estimate=pl.CostEstimate(
            flops=2 * stencil.size * bins * k, bytes_accessed=4_000_000, transcendentals=0
        ),
    )(depart_slot.reshape(-1), stencil, wind, pool)


def step_kernel(
    sizes,
    spec_ref,
    val_ref,
    slope_ref,
    factor_ref,
    old_ref,
    weight_ref,
    cos_ref,
    sin_ref,
    table_ref,
    start_ref,
    points_ref,
    wind_ref,
    pool,
    stencil,
    spec,
    val,
    slope,
    old,
    low,
    high,
    below,
    above,
    outgoing,
    acc,
    terms_out,
    terms_in,
    lhs,
    grid,
    load_sem,
    halo_send,
    halo_recv,
    term_send,
    term_recv,
    block_send,
    block_recv,
):
    bands, levs, offsets, slots = sizes
    band, lev = lax.axis_index("band"), lax.axis_index("lev")
    _, bins, k, _ = old.shape
    block_count = wind_ref.shape[2] // BLK
    rows = bins * k
    reach = offsets // 2

    loads = [
        pltpu.make_async_copy(source, target, load_sem.at[i])
        for i, (source, target) in enumerate(
            [(old_ref, old), (spec_ref, spec), (val_ref, val), (slope_ref, slope)]
        )
    ]
    for load in loads:
        load.start()

    barrier = pltpu.get_barrier_semaphore()
    for d in range(1, bands):
        peer = lax.rem(band + d, bands)
        pl.semaphore_signal(barrier, inc=1, device_id={"band": peer}, device_id_type=MESH)
    after = lax.rem(lev + 1, levs)
    before = lax.rem(lev + levs - 1, levs)

    for beside in (after, before):
        pl.semaphore_signal(barrier, inc=1, device_id={"lev": beside}, device_id_type=MESH)

    loads[0].wait()

    def edges(slot, carry):
        whole = old[slot].astype(jnp.float32)
        low[slot] = whole[:, 0, :].astype(jnp.bfloat16)
        high[slot] = whole[:, k - 1, :].astype(jnp.bfloat16)
        return carry

    lax.fori_loop(0, offsets * slots, edges, 0)

    @pl.when(lev == 0)
    def _():
        below[...] = jnp.zeros_like(below)

    @pl.when(lev == levs - 1)
    def _():
        above[...] = jnp.zeros_like(above)

    pl.semaphore_wait(barrier, bands + 1)

    up = pltpu.make_async_remote_copy(
        src_ref=high,
        dst_ref=below,
        send_sem=halo_send.at[0],
        recv_sem=halo_recv.at[0],
        device_id={"lev": after},
        device_id_type=MESH,
    )
    down = pltpu.make_async_remote_copy(
        src_ref=low,
        dst_ref=above,
        send_sem=halo_send.at[1],
        recv_sem=halo_recv.at[1],
        device_id={"lev": before},
        device_id_type=MESH,
    )

    @pl.when(lev < levs - 1)
    def _():
        up.start()

    @pl.when(lev > 0)
    def _():
        down.start()

    stencil_rows = start_ref.shape[1]
    points = points_ref.shape[2]
    q = lax.broadcasted_iota(jnp.int32, (BLK, BLK), 0)

    def build(c, carry):
        starts = start_ref[c]
        for t in range(stencil_rows):
            away = q - starts[t : t + 1, :]
            weights = points_ref[c, t].astype(jnp.float32)
            matrix = jnp.zeros((BLK, BLK), jnp.float32)
            for u in range(points):
                matrix = jnp.where(away == u, weights[u : u + 1, :], matrix)
            stencil[c, t * BLK : (t + 1) * BLK, :] = matrix.astype(jnp.bfloat16)
        return carry

    lax.fori_loop(0, block_count, build, 0)

    @pl.when(lev > 0)
    def _():
        up.wait_recv()

    @pl.when(lev < levs - 1)
    def _():
        down.wait_recv()

    level = lax.broadcasted_iota(jnp.int32, (1, k, BLK), 1)

    def remapped(slot):
        weights = weight_ref[slot].astype(jnp.float32)
        here = old[slot].astype(jnp.float32)
        under = below[slot].astype(jnp.float32)[:, None, :]
        over = above[slot].astype(jnp.float32)[:, None, :]
        lower = jnp.where(level == 0, under, pltpu.roll(here, 1, 1))
        upper = jnp.where(level == k - 1, over, pltpu.roll(here, k - 1, 1))
        summed = weights[0:1] * lower + weights[1:2] * here + weights[2:3] * upper
        return summed.reshape(rows, BLK).astype(jnp.bfloat16)

    copies = []
    for o in sorted(range(offsets), key=lambda o: (-abs(o - reach), o)):

        def fill(e, carry, o=o):
            outgoing[o * slots + e] = remapped(o * slots + e)
            return carry

        lax.fori_loop(0, slots, fill, 0)
        at = pl.ds(o * slots, slots)
        if o == reach:
            kept = pltpu.make_async_copy(outgoing.at[at], pool.at[at], load_sem.at[4])
            kept.start()
            continue
        to, source = band + (o - reach), band - (o - reach)
        copy = pltpu.make_async_remote_copy(
            src_ref=outgoing.at[at],
            dst_ref=pool.at[at],
            send_sem=block_send.at[o],
            recv_sem=block_recv.at[o],
            device_id={"band": lax.rem(to + bands, bands)},
            device_id_type=MESH,
        )
        sends = (to >= 0) & (to < bands)
        receives = (source >= 0) & (source < bands)
        copies.append((copy, sends, receives))

        @pl.when(sends)
        def _(copy=copy):
            copy.start()

    for load in loads[1:]:
        load.wait()
    fields = spec.shape[0]
    lat_count = val.shape[1]
    trunc = spec.shape[2]
    cols = GROUP * lat_count
    width = acc.shape[1]
    lanes = width // lat_count
    own = lax.broadcasted_iota(jnp.int32, (GROUP, cols), 0)
    col = lax.broadcasted_iota(jnp.int32, (GROUP, cols), 1)
    keep = (col // lat_count == own)[None]
    row = lax.broadcasted_iota(jnp.int32, (cols, width), 0)
    lane = lax.broadcasted_iota(jnp.int32, (cols, width), 1)
    acc[...] = jnp.zeros_like(acc)

    def transform(g, carry):
        at = pl.ds(pl.multiple_of(g * GROUP, GROUP), GROUP)
        left = spec[:, at, :].reshape(fields * GROUP, trunc)

        def terms(table):
            right = table[at].reshape(cols, trunc)
            product = lax.dot_general(
                left, right, (((1,), (1,)), ((), ())), preferred_element_type=jnp.float32
            ).reshape(fields, GROUP, cols)
            return jnp.sum(jnp.where(keep, product, 0.0), axis=1)

        value, tilt = terms(val), terms(slope)
        factor = factor_ref[g]
        v = [value[x * k : (x + 1) * k] for x in range(4)]
        d = [tilt[x * k : (x + 1) * k] for x in range(4)]
        coefficients = jnp.concatenate(
            [
                -d[0] - factor * v[3],
                -d[1] + factor * v[2],
                d[2] - factor * v[1],
                d[3] + factor * v[0],
            ],
            axis=0,
        ).astype(jnp.bfloat16)
        slot = lane % lanes - g * GROUP
        hot = (slot * lat_count + lane // lanes == row) & (slot >= 0) & (slot < GROUP)
        hot = hot.astype(jnp.float32).astype(jnp.bfloat16)
        acc[...] += jnp.dot(coefficients, hot, preferred_element_type=jnp.float32)
        return carry

    lax.fori_loop(0, spec.shape[1] // GROUP, transform, 0)
    for lat in range(lat_count):
        terms_out[lat] = acc[:, lat * lanes : (lat + 1) * lanes].astype(jnp.bfloat16)
    exchanges = []
    for d in range(1, bands):
        peer = lax.rem(band + d, bands)
        copy = pltpu.make_async_remote_copy(
            src_ref=terms_out.at[peer],
            dst_ref=terms_in.at[band],
            send_sem=term_send.at[d],
            recv_sem=term_recv.at[d],
            device_id={"band": peer},
            device_id_type=MESH,
        )
        copy.start()
        exchanges.append(copy)
    terms_in[band] = terms_out[band]
    for copy in exchanges:
        copy.wait()

    whole = jnp.concatenate([terms_in[b] for b in range(bands)], axis=1).astype(jnp.float32)
    real = jnp.concatenate([whole[0:k], whole[2 * k : 3 * k]], axis=0)
    imag = jnp.concatenate([whole[k : 2 * k], whole[3 * k : 4 * k]], axis=0)
    span = whole.shape[1]

    def turn(c, carry):
        cos_c = cos_ref[pl.ds(c, 1), :]
        sin_c = sin_ref[pl.ds(c, 1), :]
        at = pl.ds(pl.multiple_of(c * 2 * k, 2 * k), 2 * k)
        lhs[at, 0:span] = (real * cos_c - imag * sin_c).astype(jnp.bfloat16)
        lhs[at, span : 2 * span] = (-real * sin_c - imag * cos_c).astype(jnp.bfloat16)
        return carry

    lax.fori_loop(0, block_count, turn, 0)
    grid[...] = jnp.dot(lhs[...], table_ref[...], preferred_element_type=jnp.float32)
    for c in range(block_count):
        for w in range(2):
            start = (2 * c + w) * k
            wind_ref[w, :, c * BLK : (c + 1) * BLK] = grid[start : start + k].astype(jnp.bfloat16)

    kept.wait()
    for copy, sends, receives in copies:

        @pl.when(receives)
        def _(copy=copy):
            copy.wait_recv()

    for copy, sends, receives in copies:

        @pl.when(sends)
        def _(copy=copy):
            copy.wait_send()

    @pl.when(lev < levs - 1)
    def _():
        up.wait_send()

    @pl.when(lev > 0)
    def _():
        down.wait_send()


def shards(
    spectral,
    legendre_value,
    legendre_slope,
    wave_numbers,
    aerosol_old,
    vertical_weight,
    send_blocks,
    depart_slot,
    depart_offset,
    depart_weight,
):
    band_here = lax.axis_index("band")
    bands, levs = lax.axis_size("band"), lax.axis_size("lev")
    fields, k, wave_local, trunc = spectral.shape
    bins, _, lat_here, lon_count = aerosol_old.shape
    lat_count = legendre_value.shape[1]
    block_count = lon_count // BLK
    offsets, slots = send_blocks.shape[1:]
    rows = fields * k
    old = aerosol_old.reshape(bins, k, lon_count)
    weight = vertical_weight.reshape(3, k, lon_count)

    own_waves = lax.dynamic_slice_in_dim(wave_numbers, band_here * wave_local, wave_local, 0)
    spec = padded_to(spectral.reshape(rows, wave_local, trunc), 1, GROUP)
    value = padded_to(legendre_value, 0, GROUP)
    slope = padded_to(legendre_slope, 0, GROUP)
    steps = spec.shape[1] // GROUP
    lanes = -(-spec.shape[1] // LANES) * LANES
    factor = padded_to(own_waves.astype(jnp.float32) / WAVES, 0, GROUP)
    factor = jnp.broadcast_to(factor[:, None], (factor.shape[0], lat_count))
    factor = factor.reshape(steps, 1, GROUP * lat_count)
    cos_block, sin_block, table = angle_tables(wave_numbers, bands, lanes, block_count)

    edge = pltpu.VMEM((offsets * slots, bins, BLK), jnp.bfloat16)
    blocks = pltpu.VMEM((offsets * slots, bins * k, BLK), jnp.bfloat16)
    terms = pltpu.VMEM((bands, rows, lanes), jnp.bfloat16)
    dma = pltpu.SemaphoreType.DMA
    listed, listed_weight = listed_blocks(send_blocks.reshape(-1), old, weight)
    wind, pool, stencil = pl.pallas_call(
        functools.partial(step_kernel, (bands, levs, offsets, slots)),
        out_shape=[
            jax.ShapeDtypeStruct((2, k, lon_count), jnp.bfloat16),
            jax.ShapeDtypeStruct((offsets * slots, bins * k, BLK), jnp.bfloat16),
            jax.ShapeDtypeStruct((block_count, depart_slot.shape[1] * BLK, BLK), jnp.bfloat16),
        ],
        in_specs=[ANY, ANY, ANY, VMEM, ANY] + [VMEM] * 6,
        out_specs=[VMEM, ANY, VMEM],
        scratch_shapes=[
            pltpu.VMEM(spec.shape, jnp.bfloat16),
            pltpu.VMEM(value.shape, jnp.bfloat16),
            pltpu.VMEM(slope.shape, jnp.bfloat16),
            pltpu.VMEM(listed.shape, jnp.bfloat16),
            edge,
            edge,
            edge,
            edge,
            blocks,
            pltpu.VMEM((rows, lat_count * lanes), jnp.float32),
            terms,
            terms,
            pltpu.VMEM((block_count * 2 * k, table.shape[0]), jnp.bfloat16),
            pltpu.VMEM((block_count * 2 * k, BLK), jnp.float32),
            dma((5,)),
            dma((2,)),
            dma((2,)),
            dma((bands,)),
            dma((bands,)),
            dma((offsets,)),
            dma((offsets,)),
        ],
        compiler_params=pltpu.CompilerParams(
            collective_id=0, has_side_effects=True, vmem_limit_bytes=LIMIT
        ),
        cost_estimate=pl.CostEstimate(
            flops=4_000_000_000, bytes_accessed=10_000_000, transcendentals=0
        ),
    )(
        spec,
        value,
        slope,
        factor,
        listed,
        listed_weight,
        cos_block,
        sin_block,
        table,
        depart_offset,
        depart_weight,
    )
    new, flux = arrivals(depart_slot, stencil, wind, pool, bins)
    lat_shape = (k, lat_here, lon_count)
    return (
        wind.reshape((2, *lat_shape)),
        new.reshape((bins, *lat_shape)),
        flux.reshape((2, *lat_shape)),
    )


def solution(mesh):
    return jax.shard_map(
        shards,
        mesh=mesh,
        in_specs=(
            P(None, "lev", "band", None),
            P("band", None, None),
            P("band", None, None),
            P(),
            P(None, "lev", "band", None),
            P(None, "lev", "band", None),
            P("band", None, None),
            P("band", None),
            P("band", None, None),
            P("band", None, None, None),
        ),
        out_specs=(
            P(None, "lev", "band", None),
            P(None, "lev", "band", None),
            P(None, "lev", "band", None),
        ),
        check_vma=False,
    )
```

```python
import functools
import math

import jax
import jax.numpy as jnp
from jax import lax
from jax.experimental import pallas as pl
from jax.experimental.pallas import tpu as pltpu
from jax.sharding import PartitionSpec as P

WAVES = 640
NLON = 2688
BLK = 128
GROUP = 16
LANES = 128
FINE = 16
LIMIT = 16 * 2**20
VMEM = pl.BlockSpec(memory_space=pltpu.VMEM)
SMEM = pl.BlockSpec(memory_space=pltpu.SMEM)


ANY = pl.BlockSpec(memory_space=pl.ANY)
MESH = pl.DeviceIdType.MESH


def padded_to(value, axis, multiple):
    extra = -value.shape[axis] % multiple
    if extra == 0:
        return value
    widths = [(0, 0)] * value.ndim
    widths[axis] = (0, extra)
    return jnp.pad(value, widths)


def block_of(index):
    return pl.ds(pl.multiple_of(index * BLK, BLK), BLK)


def gather_kernel(listed_ref, old_ref, weight_ref, blocks_ref, weights_ref):
    block_count = old_ref.shape[2] // BLK

    def take(slot, carry):
        lons = block_of(jnp.clip(listed_ref[slot], 0, block_count - 1))
        blocks_ref[slot] = old_ref[:, :, lons]
        weights_ref[slot] = weight_ref[:, :, lons]
        return carry

    lax.fori_loop(0, blocks_ref.shape[0], take, 0)


def listed_blocks(listed, old, weight):
    count = listed.shape[0]
    bins, k, _ = old.shape
    return pl.pallas_call(
        gather_kernel,
        out_shape=[
            jax.ShapeDtypeStruct((count, bins, k, BLK), jnp.bfloat16),
            jax.ShapeDtypeStruct((count, 3, k, BLK), jnp.bfloat16),
        ],
        in_specs=[SMEM, VMEM, VMEM],
        out_specs=[VMEM, VMEM],
        compiler_params=pltpu.CompilerParams(vmem_limit_bytes=LIMIT),
    )(listed, old, weight)


def arrive_kernel(depart_ref, stencil_ref, wind_ref, pool_ref, new_ref, flux_ref):
    bins, k, lon_count = new_ref.shape
    block_count, depth, _ = stencil_ref.shape
    stencil_rows = depth // BLK

    def arrive(c, carry):
        taken = [pool_ref[depart_ref[c * stencil_rows + t]] for t in range(stencil_rows)]
        new = jnp.dot(
            jnp.concatenate(taken, axis=1), stencil_ref[c], preferred_element_type=jnp.float32
        )
        new = new.astype(jnp.bfloat16).astype(jnp.float32).reshape(bins, k, BLK)
        lons = block_of(c)
        new_ref[:, :, lons] = new.astype(jnp.bfloat16)
        average = jnp.sum(new, axis=0) / bins
        wind = wind_ref[:, :, lons].astype(jnp.float32)
        flux_ref[:, :, lons] = (wind * average[None]).astype(jnp.bfloat16)
        return carry

    lax.fori_loop(0, block_count, arrive, 0)


def arrivals(depart_slot, stencil, wind, pool, bins):
    _, k, lon_count = wind.shape
    return pl.pallas_call(
        arrive_kernel,
        out_shape=[
            jax.ShapeDtypeStruct((bins, k, lon_count), jnp.bfloat16),
            jax.ShapeDtypeStruct((2, k, lon_count), jnp.bfloat16),
        ],
        in_specs=[SMEM] + [VMEM] * 3,
        out_specs=[VMEM, VMEM],
        compiler_params=pltpu.CompilerParams(vmem_limit_bytes=LIMIT),
        cost_estimate=pl.CostEstimate(
            flops=2 * stencil.size * bins * k, bytes_accessed=4_000_000, transcendentals=0
        ),
    )(depart_slot.reshape(-1), stencil, wind, pool)


def step_kernel(
    sizes,
    spec_ref,
    val_ref,
    slope_ref,
    factor_ref,
    old_ref,
    weight_ref,
    waves_ref,
    start_ref,
    points_ref,
    wind_ref,
    pool,
    stencil,
    spec,
    val,
    slope,
    old,
    low,
    high,
    below,
    above,
    outgoing,
    acc,
    terms_out,
    terms_in,
    lhs,
    grid,
    cos_ref,
    sin_ref,
    table,
    load_sem,
    halo_send,
    halo_recv,
    term_send,
    term_recv,
    block_send,
    block_recv,
):
    bands, levs, offsets, slots = sizes
    band, lev = lax.axis_index("band"), lax.axis_index("lev")
    _, bins, k, _ = old.shape
    block_count = wind_ref.shape[2] // BLK
    rows = bins * k
    reach = offsets // 2

    loads = [
        pltpu.make_async_copy(source, target, load_sem.at[i])
        for i, (source, target) in enumerate(
            [(old_ref, old), (spec_ref, spec), (val_ref, val), (slope_ref, slope)]
        )
    ]
    for load in loads:
        load.start()

    barrier = pltpu.get_barrier_semaphore()
    for d in range(1, bands):
        peer = lax.rem(band + d, bands)
        pl.semaphore_signal(barrier, inc=1, device_id={"band": peer}, device_id_type=MESH)
    after = lax.rem(lev + 1, levs)
    before = lax.rem(lev + levs - 1, levs)

    for beside in (after, before):
        pl.semaphore_signal(barrier, inc=1, device_id={"lev": beside}, device_id_type=MESH)

    loads[0].wait()

    def edges(slot, carry):
        whole = old[slot].astype(jnp.float32)
        low[slot] = whole[:, 0, :].astype(jnp.bfloat16)
        high[slot] = whole[:, k - 1, :].astype(jnp.bfloat16)
        return carry

    lax.fori_loop(0, offsets * slots, edges, 0)

    @pl.when(lev == 0)
    def _():
        below[...] = jnp.zeros_like(below)

    @pl.when(lev == levs - 1)
    def _():
        above[...] = jnp.zeros_like(above)

    pl.semaphore_wait(barrier, bands + 1)

    up = pltpu.make_async_remote_copy(
        src_ref=high,
        dst_ref=below,
        send_sem=halo_send.at[0],
        recv_sem=halo_recv.at[0],
        device_id={"lev": after},
        device_id_type=MESH,
    )
    down = pltpu.make_async_remote_copy(
        src_ref=low,
        dst_ref=above,
        send_sem=halo_send.at[1],
        recv_sem=halo_recv.at[1],
        device_id={"lev": before},
        device_id_type=MESH,
    )

    @pl.when(lev < levs - 1)
    def _():
        up.start()

    @pl.when(lev > 0)
    def _():
        down.start()

    stencil_rows = start_ref.shape[1]
    points = points_ref.shape[2]
    q = lax.broadcasted_iota(jnp.int32, (BLK, BLK), 0)

    def build(c, carry):
        starts = start_ref[c]
        for t in range(stencil_rows):
            away = q - starts[t : t + 1, :]
            weights = points_ref[c, t].astype(jnp.float32)
            matrix = jnp.zeros((BLK, BLK), jnp.float32)
            for u in range(points):
                matrix = jnp.where(away == u, weights[u : u + 1, :], matrix)
            stencil[c, t * BLK : (t + 1) * BLK, :] = matrix.astype(jnp.bfloat16)
        return carry

    lax.fori_loop(0, block_count, build, 0)

    @pl.when(lev > 0)
    def _():
        up.wait_recv()

    @pl.when(lev < levs - 1)
    def _():
        down.wait_recv()

    level = lax.broadcasted_iota(jnp.int32, (1, k, BLK), 1)

    def remapped(slot):
        weights = weight_ref[slot].astype(jnp.float32)
        here = old[slot].astype(jnp.float32)
        under = below[slot].astype(jnp.float32)[:, None, :]
        over = above[slot].astype(jnp.float32)[:, None, :]
        lower = jnp.where(level == 0, under, pltpu.roll(here, 1, 1))
        upper = jnp.where(level == k - 1, over, pltpu.roll(here, k - 1, 1))
        summed = weights[0:1] * lower + weights[1:2] * here + weights[2:3] * upper
        return summed.reshape(rows, BLK).astype(jnp.bfloat16)

    copies = []
    for o in sorted(range(offsets), key=lambda o: (-abs(o - reach), o)):

        def fill(e, carry, o=o):
            outgoing[o * slots + e] = remapped(o * slots + e)
            return carry

        lax.fori_loop(0, slots, fill, 0)
        at = pl.ds(o * slots, slots)
        if o == reach:
            kept = pltpu.make_async_copy(outgoing.at[at], pool.at[at], load_sem.at[4])
            kept.start()
            continue
        to, source = band + (o - reach), band - (o - reach)
        copy = pltpu.make_async_remote_copy(
            src_ref=outgoing.at[at],
            dst_ref=pool.at[at],
            send_sem=block_send.at[o],
            recv_sem=block_recv.at[o],
            device_id={"band": lax.rem(to + bands, bands)},
            device_id_type=MESH,
        )
        sends = (to >= 0) & (to < bands)
        receives = (source >= 0) & (source < bands)
        copies.append((copy, sends, receives))

        @pl.when(sends)
        def _(copy=copy):
            copy.start()

    for load in loads[1:]:
        load.wait()
    fields = spec.shape[0]
    lat_count = val.shape[1]
    trunc = spec.shape[2]
    cols = GROUP * lat_count
    width = acc.shape[1]
    lanes = width // lat_count
    own = lax.broadcasted_iota(jnp.int32, (GROUP, cols), 0)
    col = lax.broadcasted_iota(jnp.int32, (GROUP, cols), 1)
    keep = (col // lat_count == own)[None]
    row = lax.broadcasted_iota(jnp.int32, (cols, width), 0)
    lane = lax.broadcasted_iota(jnp.int32, (cols, width), 1)
    place = lane % lanes * lat_count + lane // lanes - row
    acc[...] = jnp.zeros_like(acc)

    def transform(g, carry):
        at = pl.ds(pl.multiple_of(g * GROUP, GROUP), GROUP)
        left = spec[:, at, :].reshape(fields * GROUP, trunc)

        def terms(table):
            right = table[at].reshape(cols, trunc)
            product = lax.dot_general(
                left, right, (((1,), (1,)), ((), ())), preferred_element_type=jnp.float32
            ).reshape(fields, GROUP, cols)
            return jnp.sum(jnp.where(keep, product, 0.0), axis=1)

        value, tilt = terms(val), terms(slope)
        factor = factor_ref[g]
        v = [value[x * k : (x + 1) * k] for x in range(4)]
        d = [tilt[x * k : (x + 1) * k] for x in range(4)]
        coefficients = jnp.concatenate(
            [
                -d[0] - factor * v[3],
                -d[1] + factor * v[2],
                d[2] - factor * v[1],
                d[3] + factor * v[0],
            ],
            axis=0,
        ).astype(jnp.bfloat16)
        hot = (place == g * cols).astype(jnp.float32).astype(jnp.bfloat16)
        acc[...] += jnp.dot(coefficients, hot, preferred_element_type=jnp.float32)
        return carry

    lax.fori_loop(0, spec.shape[1] // GROUP, transform, 0)
    for lat in range(lat_count):
        terms_out[lat] = acc[:, lat * lanes : (lat + 1) * lanes].astype(jnp.bfloat16)
    exchanges = []
    for d in range(1, bands):
        peer = lax.rem(band + d, bands)
        copy = pltpu.make_async_remote_copy(
            src_ref=terms_out.at[peer],
            dst_ref=terms_in.at[band],
            send_sem=term_send.at[d],
            recv_sem=term_recv.at[d],
            device_id={"band": peer},
            device_id_type=MESH,
        )
        copy.start()
        exchanges.append(copy)
    terms_in[band] = terms_out[band]

    waves = waves_ref[...]
    span = waves.shape[1]

    def angles(count, stride):
        turns = lax.broadcasted_iota(jnp.int32, (count, span), 0) * stride
        turns = lax.rem(turns * waves, NLON).astype(jnp.float32) * (2.0 * math.pi / NLON)
        return jnp.cos(turns), jnp.sin(turns)

    doubled = jnp.where(waves == 0, 1.0, 2.0)
    cos_c, sin_c = angles(cos_ref.shape[0], BLK)
    cos_ref[...] = doubled * cos_c
    sin_ref[...] = doubled * sin_c
    cos_a, sin_a = angles(BLK // FINE, FINE)
    cos_b, sin_b = angles(FINE, 1)
    for a in range(BLK // FINE):
        ca, sa = cos_a[a : a + 1], sin_a[a : a + 1]
        at = slice(a * FINE, (a + 1) * FINE)
        table[at, 0:span] = (ca * cos_b - sa * sin_b).astype(jnp.bfloat16)
        table[at, span : 2 * span] = (sa * cos_b + ca * sin_b).astype(jnp.bfloat16)
    for copy in exchanges:
        copy.wait()

    whole = jnp.concatenate([terms_in[b] for b in range(bands)], axis=1).astype(jnp.float32)
    real = jnp.concatenate([whole[0:k], whole[2 * k : 3 * k]], axis=0)
    imag = jnp.concatenate([whole[k : 2 * k], whole[3 * k : 4 * k]], axis=0)

    def turn(c, carry):
        cos_c = cos_ref[pl.ds(c, 1), :]
        sin_c = sin_ref[pl.ds(c, 1), :]
        at = pl.ds(pl.multiple_of(c * 2 * k, 2 * k), 2 * k)
        lhs[at, 0:span] = (real * cos_c - imag * sin_c).astype(jnp.bfloat16)
        lhs[at, span : 2 * span] = (-real * sin_c - imag * cos_c).astype(jnp.bfloat16)
        return carry

    lax.fori_loop(0, block_count, turn, 0)
    grid[...] = lax.dot_general(
        lhs[...], table[...], (((1,), (1,)), ((), ())), preferred_element_type=jnp.float32
    )
    for c in range(block_count):
        for w in range(2):
            start = (2 * c + w) * k
            wind_ref[w, :, c * BLK : (c + 1) * BLK] = grid[start : start + k].astype(jnp.bfloat16)

    kept.wait()
    for copy, sends, receives in copies:

        @pl.when(receives)
        def _(copy=copy):
            copy.wait_recv()

    for copy, sends, receives in copies:

        @pl.when(sends)
        def _(copy=copy):
            copy.wait_send()

    @pl.when(lev < levs - 1)
    def _():
        up.wait_send()

    @pl.when(lev > 0)
    def _():
        down.wait_send()


def shards(
    spectral,
    legendre_value,
    legendre_slope,
    wave_numbers,
    aerosol_old,
    vertical_weight,
    send_blocks,
    depart_slot,
    depart_offset,
    depart_weight,
):
    band_here = lax.axis_index("band")
    bands, levs = lax.axis_size("band"), lax.axis_size("lev")
    fields, k, wave_local, trunc = spectral.shape
    bins, _, lat_here, lon_count = aerosol_old.shape
    lat_count = legendre_value.shape[1]
    block_count = lon_count // BLK
    offsets, slots = send_blocks.shape[1:]
    rows = fields * k
    old = aerosol_old.reshape(bins, k, lon_count)
    weight = vertical_weight.reshape(3, k, lon_count)

    own_waves = lax.dynamic_slice_in_dim(wave_numbers, band_here * wave_local, wave_local, 0)
    spec = padded_to(spectral.reshape(rows, wave_local, trunc), 1, GROUP)
    value = padded_to(legendre_value, 0, GROUP)
    slope = padded_to(legendre_slope, 0, GROUP)
    steps = spec.shape[1] // GROUP
    lanes = -(-spec.shape[1] // LANES) * LANES
    factor = padded_to(own_waves.astype(jnp.float32) / WAVES, 0, GROUP)
    factor = jnp.broadcast_to(factor[:, None], (factor.shape[0], lat_count))
    factor = factor.reshape(steps, 1, GROUP * lat_count)
    waves = padded_to(wave_numbers.reshape(bands, wave_local), 1, lanes).reshape(1, -1)
    span = bands * lanes
    coarse = pltpu.VMEM((-(-block_count // 8) * 8, span), jnp.float32)

    edge = pltpu.VMEM((offsets * slots, bins, BLK), jnp.bfloat16)
    blocks = pltpu.VMEM((offsets * slots, bins * k, BLK), jnp.bfloat16)
    terms = pltpu.VMEM((bands, rows, lanes), jnp.bfloat16)
    dma = pltpu.SemaphoreType.DMA
    listed, listed_weight = listed_blocks(send_blocks.reshape(-1), old, weight)
    wind, pool, stencil = pl.pallas_call(
        functools.partial(step_kernel, (bands, levs, offsets, slots)),
        out_shape=[
            jax.ShapeDtypeStruct((2, k, lon_count), jnp.bfloat16),
            jax.ShapeDtypeStruct((offsets * slots, bins * k, BLK), jnp.bfloat16),
            jax.ShapeDtypeStruct((block_count, depart_slot.shape[1] * BLK, BLK), jnp.bfloat16),
        ],
        in_specs=[ANY, ANY, ANY, VMEM, ANY] + [VMEM] * 4,
        out_specs=[VMEM, ANY, VMEM],
        scratch_shapes=[
            pltpu.VMEM(spec.shape, jnp.bfloat16),
            pltpu.VMEM(value.shape, jnp.bfloat16),
            pltpu.VMEM(slope.shape, jnp.bfloat16),
            pltpu.VMEM(listed.shape, jnp.bfloat16),
            edge,
            edge,
            edge,
            edge,
            blocks,
            pltpu.VMEM((rows, lat_count * lanes), jnp.float32),
            terms,
            terms,
            pltpu.VMEM((block_count * 2 * k, 2 * span), jnp.bfloat16),
            pltpu.VMEM((block_count * 2 * k, BLK), jnp.float32),
            coarse,
            coarse,
            pltpu.VMEM((BLK, 2 * span), jnp.bfloat16),
            dma((5,)),
            dma((2,)),
            dma((2,)),
            dma((bands,)),
            dma((bands,)),
            dma((offsets,)),
            dma((offsets,)),
        ],
        compiler_params=pltpu.CompilerParams(
            collective_id=0, has_side_effects=True, vmem_limit_bytes=(44 + bands // 8) * 2**20
        ),
        cost_estimate=pl.CostEstimate(
            flops=4_000_000_000, bytes_accessed=10_000_000, transcendentals=0
        ),
    )(
        spec,
        value,
        slope,
        factor,
        listed,
        listed_weight,
        waves,
        depart_offset,
        depart_weight,
    )
    new, flux = arrivals(depart_slot, stencil, wind, pool, bins)
    lat_shape = (k, lat_here, lon_count)
    return (
        wind.reshape((2, *lat_shape)),
        new.reshape((bins, *lat_shape)),
        flux.reshape((2, *lat_shape)),
    )


def solution(mesh):
    return jax.shard_map(
        shards,
        mesh=mesh,
        in_specs=(
            P(None, "lev", "band", None),
            P("band", None, None),
            P("band", None, None),
            P(),
            P(None, "lev", "band", None),
            P(None, "lev", "band", None),
            P("band", None, None),
            P("band", None),
            P("band", None, None),
            P("band", None, None, None),
        ),
        out_specs=(
            P(None, "lev", "band", None),
            P(None, "lev", "band", None),
            P(None, "lev", "band", None),
        ),
        check_vma=False,
    )
```

```python
import functools
import math

import jax
import jax.numpy as jnp
from jax import lax
from jax.experimental import pallas as pl
from jax.experimental.pallas import tpu as pltpu
from jax.sharding import PartitionSpec as P

WAVES = 640
NLON = 2688
BLK = 128
GROUP = 16
LANES = 128
FINE = 16
LIMIT = 16 * 2**20
VMEM = pl.BlockSpec(memory_space=pltpu.VMEM)
SMEM = pl.BlockSpec(memory_space=pltpu.SMEM)


ANY = pl.BlockSpec(memory_space=pl.ANY)
MESH = pl.DeviceIdType.MESH


def padded_to(value, axis, multiple):
    extra = -value.shape[axis] % multiple
    if extra == 0:
        return value
    widths = [(0, 0)] * value.ndim
    widths[axis] = (0, extra)
    return jnp.pad(value, widths)


def block_of(index):
    return pl.ds(pl.multiple_of(index * BLK, BLK), BLK)


def gather_kernel(listed_ref, old_ref, weight_ref, blocks_ref, weights_ref):
    block_count = old_ref.shape[2] // BLK
    slots = listed_ref.shape[0]

    def take(slot, carry):
        lons = block_of(jnp.clip(listed_ref[slot % slots, slot // slots], 0, block_count - 1))
        blocks_ref[slot] = old_ref[:, :, lons]
        weights_ref[slot] = weight_ref[:, :, lons]
        return carry

    lax.fori_loop(0, blocks_ref.shape[0], take, 0)


def listed_blocks(listed, old, weight):
    count = listed.size
    bins, k, _ = old.shape
    return pl.pallas_call(
        gather_kernel,
        out_shape=[
            jax.ShapeDtypeStruct((count, bins, k, BLK), jnp.bfloat16),
            jax.ShapeDtypeStruct((count, 3, k, BLK), jnp.bfloat16),
        ],
        in_specs=[SMEM, VMEM, VMEM],
        out_specs=[VMEM, VMEM],
        compiler_params=pltpu.CompilerParams(vmem_limit_bytes=LIMIT),
    )(listed, old, weight)


def arrive_kernel(depart_ref, stencil_ref, wind_ref, pool_ref, new_ref, flux_ref):
    bins, k, lon_count = new_ref.shape
    block_count, depth, _ = stencil_ref.shape
    stencil_rows = depth // BLK

    def arrive(c, carry):
        taken = [pool_ref[depart_ref[t, c]] for t in range(stencil_rows)]
        new = jnp.dot(
            jnp.concatenate(taken, axis=1), stencil_ref[c], preferred_element_type=jnp.float32
        )
        new = new.astype(jnp.bfloat16).astype(jnp.float32).reshape(bins, k, BLK)
        lons = block_of(c)
        new_ref[:, :, lons] = new.astype(jnp.bfloat16)
        average = jnp.sum(new, axis=0) / bins
        wind = wind_ref[:, :, lons].astype(jnp.float32)
        flux_ref[:, :, lons] = (wind * average[None]).astype(jnp.bfloat16)
        return carry

    lax.fori_loop(0, block_count, arrive, 0)


def arrivals(depart_slot, stencil, wind, pool, bins):
    _, k, lon_count = wind.shape
    return pl.pallas_call(
        arrive_kernel,
        out_shape=[
            jax.ShapeDtypeStruct((bins, k, lon_count), jnp.bfloat16),
            jax.ShapeDtypeStruct((2, k, lon_count), jnp.bfloat16),
        ],
        in_specs=[SMEM] + [VMEM] * 3,
        out_specs=[VMEM, VMEM],
        compiler_params=pltpu.CompilerParams(vmem_limit_bytes=LIMIT),
        cost_estimate=pl.CostEstimate(
            flops=2 * stencil.size * bins * k, bytes_accessed=4_000_000, transcendentals=0
        ),
    )(depart_slot.T, stencil, wind, pool)


def step_kernel(
    sizes,
    spec_ref,
    val_ref,
    slope_ref,
    factor_ref,
    old_ref,
    weight_ref,
    waves_ref,
    start_ref,
    points_ref,
    wind_ref,
    pool,
    stencil,
    spec,
    val,
    slope,
    old,
    low,
    high,
    below,
    above,
    outgoing,
    acc,
    terms_out,
    terms_in,
    lhs,
    grid,
    cos_ref,
    sin_ref,
    table,
    load_sem,
    halo_send,
    halo_recv,
    term_send,
    term_recv,
    block_send,
    block_recv,
):
    bands, levs, offsets, slots = sizes
    band, lev = lax.axis_index("band"), lax.axis_index("lev")
    _, bins, k, _ = old.shape
    block_count = wind_ref.shape[2] // BLK
    rows = bins * k
    reach = offsets // 2

    loads = [
        pltpu.make_async_copy(source, target, load_sem.at[i])
        for i, (source, target) in enumerate(
            [(old_ref, old), (spec_ref, spec), (val_ref, val), (slope_ref, slope)]
        )
    ]
    for load in loads:
        load.start()

    barrier = pltpu.get_barrier_semaphore()
    for d in range(1, bands):
        peer = lax.rem(band + d, bands)
        pl.semaphore_signal(barrier, inc=1, device_id={"band": peer}, device_id_type=MESH)
    after = lax.rem(lev + 1, levs)
    before = lax.rem(lev + levs - 1, levs)

    for beside in (after, before):
        pl.semaphore_signal(barrier, inc=1, device_id={"lev": beside}, device_id_type=MESH)

    loads[0].wait()

    def edges(slot, carry):
        whole = old[slot].astype(jnp.float32)
        low[slot] = whole[:, 0, :].astype(jnp.bfloat16)
        high[slot] = whole[:, k - 1, :].astype(jnp.bfloat16)
        return carry

    lax.fori_loop(0, offsets * slots, edges, 0)

    @pl.when(lev == 0)
    def _():
        below[...] = jnp.zeros_like(below)

    @pl.when(lev == levs - 1)
    def _():
        above[...] = jnp.zeros_like(above)

    pl.semaphore_wait(barrier, bands + 1)

    up = pltpu.make_async_remote_copy(
        src_ref=high,
        dst_ref=below,
        send_sem=halo_send.at[0],
        recv_sem=halo_recv.at[0],
        device_id={"lev": after},
        device_id_type=MESH,
    )
    down = pltpu.make_async_remote_copy(
        src_ref=low,
        dst_ref=above,
        send_sem=halo_send.at[1],
        recv_sem=halo_recv.at[1],
        device_id={"lev": before},
        device_id_type=MESH,
    )

    @pl.when(lev < levs - 1)
    def _():
        up.start()

    @pl.when(lev > 0)
    def _():
        down.start()

    stencil_rows = start_ref.shape[1]
    points = points_ref.shape[2]
    q = lax.broadcasted_iota(jnp.int32, (BLK, BLK), 0)

    def build(c, carry):
        starts = start_ref[c]
        for t in range(stencil_rows):
            away = q - starts[t : t + 1, :]
            weights = points_ref[c, t].astype(jnp.float32)
            matrix = jnp.zeros((BLK, BLK), jnp.float32)
            for u in range(points):
                matrix = jnp.where(away == u, weights[u : u + 1, :], matrix)
            stencil[c, t * BLK : (t + 1) * BLK, :] = matrix.astype(jnp.bfloat16)
        return carry

    lax.fori_loop(0, block_count, build, 0)

    @pl.when(lev > 0)
    def _():
        up.wait_recv()

    @pl.when(lev < levs - 1)
    def _():
        down.wait_recv()

    level = lax.broadcasted_iota(jnp.int32, (1, k, BLK), 1)

    def remapped(slot):
        weights = weight_ref[slot].astype(jnp.float32)
        here = old[slot].astype(jnp.float32)
        under = below[slot].astype(jnp.float32)[:, None, :]
        over = above[slot].astype(jnp.float32)[:, None, :]
        lower = jnp.where(level == 0, under, pltpu.roll(here, 1, 1))
        upper = jnp.where(level == k - 1, over, pltpu.roll(here, k - 1, 1))
        summed = weights[0:1] * lower + weights[1:2] * here + weights[2:3] * upper
        return summed.reshape(rows, BLK).astype(jnp.bfloat16)

    copies = []
    for o in sorted(range(offsets), key=lambda o: (-abs(o - reach), o)):

        def fill(e, carry, o=o):
            outgoing[o * slots + e] = remapped(o * slots + e)
            return carry

        lax.fori_loop(0, slots, fill, 0)
        at = pl.ds(o * slots, slots)
        if o == reach:
            kept = pltpu.make_async_copy(outgoing.at[at], pool.at[at], load_sem.at[4])
            kept.start()
            continue
        to, source = band + (o - reach), band - (o - reach)
        copy = pltpu.make_async_remote_copy(
            src_ref=outgoing.at[at],
            dst_ref=pool.at[at],
            send_sem=block_send.at[o],
            recv_sem=block_recv.at[o],
            device_id={"band": lax.rem(to + bands, bands)},
            device_id_type=MESH,
        )
        sends = (to >= 0) & (to < bands)
        receives = (source >= 0) & (source < bands)
        copies.append((copy, sends, receives))

        @pl.when(sends)
        def _(copy=copy):
            copy.start()

    for load in loads[1:]:
        load.wait()
    fields = spec.shape[0]
    lat_count = val.shape[1]
    trunc = spec.shape[2]
    cols = GROUP * lat_count
    width = acc.shape[1]
    lanes = width // lat_count
    own = lax.broadcasted_iota(jnp.int32, (GROUP, cols), 0)
    col = lax.broadcasted_iota(jnp.int32, (GROUP, cols), 1)
    keep = (col // lat_count == own)[None]
    row = lax.broadcasted_iota(jnp.int32, (cols, width), 0)
    lane = lax.broadcasted_iota(jnp.int32, (cols, width), 1)
    place = lane % lanes * lat_count + lane // lanes - row
    acc[...] = jnp.zeros_like(acc)

    def transform(g, carry):
        at = pl.ds(pl.multiple_of(g * GROUP, GROUP), GROUP)
        left = spec[:, at, :].reshape(fields * GROUP, trunc)

        def terms(table):
            right = table[at].reshape(cols, trunc)
            product = lax.dot_general(
                left, right, (((1,), (1,)), ((), ())), preferred_element_type=jnp.float32
            ).reshape(fields, GROUP, cols)
            return jnp.sum(jnp.where(keep, product, 0.0), axis=1)

        value, tilt = terms(val), terms(slope)
        factor = factor_ref[g]
        v = [value[x * k : (x + 1) * k] for x in range(4)]
        d = [tilt[x * k : (x + 1) * k] for x in range(4)]
        coefficients = jnp.concatenate(
            [
                -d[0] - factor * v[3],
                -d[1] + factor * v[2],
                d[2] - factor * v[1],
                d[3] + factor * v[0],
            ],
            axis=0,
        ).astype(jnp.bfloat16)
        hot = (place == g * cols).astype(jnp.float32).astype(jnp.bfloat16)
        acc[...] += jnp.dot(coefficients, hot, preferred_element_type=jnp.float32)
        return carry

    lax.fori_loop(0, spec.shape[1] // GROUP, transform, 0)
    for lat in range(lat_count):
        terms_out[lat] = acc[:, lat * lanes : (lat + 1) * lanes].astype(jnp.bfloat16)
    exchanges = []
    for d in range(1, bands):
        peer = lax.rem(band + d, bands)
        copy = pltpu.make_async_remote_copy(
            src_ref=terms_out.at[peer],
            dst_ref=terms_in.at[band],
            send_sem=term_send.at[d],
            recv_sem=term_recv.at[d],
            device_id={"band": peer},
            device_id_type=MESH,
        )
        copy.start()
        exchanges.append(copy)
    terms_in[band] = terms_out[band]

    waves = waves_ref[...]
    span = waves.shape[1]

    def angles(count, stride):
        turns = lax.broadcasted_iota(jnp.int32, (count, span), 0) * stride
        turns = lax.rem(turns * waves, NLON).astype(jnp.float32) * (2.0 * math.pi / NLON)
        return jnp.cos(turns), jnp.sin(turns)

    doubled = jnp.where(waves == 0, 1.0, 2.0)
    cos_c, sin_c = angles(cos_ref.shape[0], BLK)
    cos_ref[...] = doubled * cos_c
    sin_ref[...] = doubled * sin_c
    cos_a, sin_a = angles(BLK // FINE, FINE)
    cos_b, sin_b = angles(FINE, 1)
    for a in range(BLK // FINE):
        ca, sa = cos_a[a : a + 1], sin_a[a : a + 1]
        at = slice(a * FINE, (a + 1) * FINE)
        table[at, 0:span] = (ca * cos_b - sa * sin_b).astype(jnp.bfloat16)
        table[at, span : 2 * span] = (sa * cos_b + ca * sin_b).astype(jnp.bfloat16)
    for copy in exchanges:
        copy.wait()

    whole = jnp.concatenate([terms_in[b] for b in range(bands)], axis=1).astype(jnp.float32)
    real = jnp.concatenate([whole[0:k], whole[2 * k : 3 * k]], axis=0)
    imag = jnp.concatenate([whole[k : 2 * k], whole[3 * k : 4 * k]], axis=0)

    def turn(c, carry):
        cos_c = cos_ref[pl.ds(c, 1), :]
        sin_c = sin_ref[pl.ds(c, 1), :]
        at = pl.ds(pl.multiple_of(c * 2 * k, 2 * k), 2 * k)
        lhs[at, 0:span] = (real * cos_c - imag * sin_c).astype(jnp.bfloat16)
        lhs[at, span : 2 * span] = (-real * sin_c - imag * cos_c).astype(jnp.bfloat16)
        return carry

    lax.fori_loop(0, block_count, turn, 0)
    grid[...] = lax.dot_general(
        lhs[...], table[...], (((1,), (1,)), ((), ())), preferred_element_type=jnp.float32
    )
    for c in range(block_count):
        for w in range(2):
            start = (2 * c + w) * k
            wind_ref[w, :, c * BLK : (c + 1) * BLK] = grid[start : start + k].astype(jnp.bfloat16)

    kept.wait()
    for copy, sends, receives in copies:

        @pl.when(receives)
        def _(copy=copy):
            copy.wait_recv()

    for copy, sends, receives in copies:

        @pl.when(sends)
        def _(copy=copy):
            copy.wait_send()

    @pl.when(lev < levs - 1)
    def _():
        up.wait_send()

    @pl.when(lev > 0)
    def _():
        down.wait_send()


def shards(
    spectral,
    legendre_value,
    legendre_slope,
    wave_numbers,
    aerosol_old,
    vertical_weight,
    send_blocks,
    depart_slot,
    depart_offset,
    depart_weight,
):
    band_here = lax.axis_index("band")
    bands, levs = lax.axis_size("band"), lax.axis_size("lev")
    fields, k, wave_local, trunc = spectral.shape
    bins, _, lat_here, lon_count = aerosol_old.shape
    lat_count = legendre_value.shape[1]
    block_count = lon_count // BLK
    offsets, slots = send_blocks.shape[1:]
    rows = fields * k
    old = aerosol_old.reshape(bins, k, lon_count)
    weight = vertical_weight.reshape(3, k, lon_count)

    own_waves = lax.dynamic_slice_in_dim(wave_numbers, band_here * wave_local, wave_local, 0)
    spec = padded_to(spectral.reshape(rows, wave_local, trunc), 1, GROUP)
    value = padded_to(legendre_value, 0, GROUP)
    slope = padded_to(legendre_slope, 0, GROUP)
    steps = spec.shape[1] // GROUP
    lanes = -(-spec.shape[1] // LANES) * LANES
    factor = padded_to(own_waves.astype(jnp.float32) / WAVES, 0, GROUP)
    factor = jnp.broadcast_to(factor[:, None], (factor.shape[0], lat_count))
    factor = factor.reshape(steps, 1, GROUP * lat_count)
    waves = padded_to(wave_numbers.reshape(bands, wave_local), 1, lanes).reshape(1, -1)
    span = bands * lanes
    coarse = pltpu.VMEM((-(-block_count // 8) * 8, span), jnp.float32)

    edge = pltpu.VMEM((offsets * slots, bins, BLK), jnp.bfloat16)
    blocks = pltpu.VMEM((offsets * slots, bins * k, BLK), jnp.bfloat16)
    terms = pltpu.VMEM((bands, rows, lanes), jnp.bfloat16)
    dma = pltpu.SemaphoreType.DMA
    listed, listed_weight = listed_blocks(send_blocks[0].T, old, weight)
    wind, pool, stencil = pl.pallas_call(
        functools.partial(step_kernel, (bands, levs, offsets, slots)),
        out_shape=[
            jax.ShapeDtypeStruct((2, k, lon_count), jnp.bfloat16),
            jax.ShapeDtypeStruct((offsets * slots, bins * k, BLK), jnp.bfloat16),
            jax.ShapeDtypeStruct((block_count, depart_slot.shape[1] * BLK, BLK), jnp.bfloat16),
        ],
        in_specs=[ANY, ANY, ANY, VMEM, ANY] + [VMEM] * 4,
        out_specs=[VMEM, ANY, VMEM],
        scratch_shapes=[
            pltpu.VMEM(spec.shape, jnp.bfloat16),
            pltpu.VMEM(value.shape, jnp.bfloat16),
            pltpu.VMEM(slope.shape, jnp.bfloat16),
            pltpu.VMEM(listed.shape, jnp.bfloat16),
            edge,
            edge,
            edge,
            edge,
            blocks,
            pltpu.VMEM((rows, lat_count * lanes), jnp.float32),
            terms,
            terms,
            pltpu.VMEM((block_count * 2 * k, 2 * span), jnp.bfloat16),
            pltpu.VMEM((block_count * 2 * k, BLK), jnp.float32),
            coarse,
            coarse,
            pltpu.VMEM((BLK, 2 * span), jnp.bfloat16),
            dma((5,)),
            dma((2,)),
            dma((2,)),
            dma((bands,)),
            dma((bands,)),
            dma((offsets,)),
            dma((offsets,)),
        ],
        compiler_params=pltpu.CompilerParams(
            collective_id=0, has_side_effects=True, vmem_limit_bytes=(44 + bands // 8) * 2**20
        ),
        cost_estimate=pl.CostEstimate(
            flops=4_000_000_000, bytes_accessed=10_000_000, transcendentals=0
        ),
    )(
        spec,
        value,
        slope,
        factor,
        listed,
        listed_weight,
        waves,
        depart_offset,
        depart_weight,
    )
    new, flux = arrivals(depart_slot, stencil, wind, pool, bins)
    lat_shape = (k, lat_here, lon_count)
    return (
        wind.reshape((2, *lat_shape)),
        new.reshape((bins, *lat_shape)),
        flux.reshape((2, *lat_shape)),
    )


def solution(mesh):
    return jax.shard_map(
        shards,
        mesh=mesh,
        in_specs=(
            P(None, "lev", "band", None),
            P("band", None, None),
            P("band", None, None),
            P(),
            P(None, "lev", "band", None),
            P(None, "lev", "band", None),
            P("band", None, None),
            P("band", None),
            P("band", None, None),
            P("band", None, None, None),
        ),
        out_specs=(
            P(None, "lev", "band", None),
            P(None, "lev", "band", None),
            P(None, "lev", "band", None),
        ),
        check_vma=False,
    )
```
